128 devices in a mesh: ma: 64 (over x, y, z_lo, core), ha: 2 (over z_hi).
Axes of the slice: x: 4, y: 4, z: 4 (z_hi: 2, z_lo: 2; z = z_hi * 2 + z_lo), core: 2. Of those that a mesh axis runs over, the one named last changes fastest.
Arguments:
- coefficients: bfloat16 [2, 1024, 10, 2, 1024], P('ha', 'ma'), may hold values from -2 to 2
- section_factors: bfloat16 [2, 1024, 64, 1024], P('ha', 'ma'), may hold values from -0.75 to 0.75
- level_factors: bfloat16 [2, 2, 1024, 64, 2048], P('ha', None, 'ma'), may hold values from -0.5 to 0.5
- partners: int32 [2, 16], replicated, may hold values from 0 to 15, as said below
- wave_ids: int32 [1024], replicated, may hold values from 0 to 1023, as said below
Outputs:
- grid: bfloat16 [2, 1024, 10, 4096], P(None, ('ma', 'ha'))
- slope: bfloat16 [2, 1024, 10, 4096], P(None, ('ma', 'ha'))
The draws below stay inside these ranges and needn't reach their ends.
Inputs may be any that keep to these rules, and one draw needn't show every extreme that they name: `partners`: row l pairs the 16 blocks: no block is its own partner, and the partner of a block's partner is the block itself. `wave_ids`: A permutation of the wavenumbers; slots 2 q and 2 q + 1 hold a wavenumber m and 1023 - m.
All inputs are finite; a program needn't handle non-finite values.
Results may differ from the reference program's by a relative error of at most 0.0075.
Values may be sent and summed in bfloat16 or wider, within the bound.
A program may use at most 192 MiB of HBM per device.

```python
import math
import jax
import jax.numpy as jnp
from jax import lax

FIELDS = 10
LATH = 1024
NLON = 4096
K = 64
LEVELS = 2
M_DEV = 16
NB = 16
M = 1024


def wave_order(key):
    inner = jax.random.fold_in(key, 23)
    low = jax.random.permutation(inner, M // 2).astype(jnp.int32)
    high = (M - 1 - low).astype(jnp.int32)
    return jnp.stack([low, high], axis=1).reshape(M)


def draw_partners(key, part):
    key = jax.random.fold_in(key, 11)
    rows = []
    for level in range(LEVELS):
        order = jax.random.permutation(jax.random.fold_in(key, level), NB).astype(jnp.int32)
        firsts = order[0::2]
        seconds = order[1::2]
        table = jnp.zeros((NB,), jnp.int32).at[firsts].set(seconds).at[seconds].set(firsts)
        rows.append(table)
    return jnp.stack(rows)


def draw_wave_ids(key, part):
    return wave_order(key)


def slot_spread(key):
    waves = wave_order(key)
    distance = (M - 1 - waves).astype(jnp.float32)
    gain = jnp.maximum(jnp.exp(-distance / 24.0), 0.01)
    return 0.5 * gain


def draw_coefficients(key, part):
    spread = slot_spread(key)
    key = jax.random.fold_in(key, 37)
    shape = (2, M, FIELDS, 2, LATH)
    values = jnp.clip(jax.random.normal(key, shape, jnp.float32), -4.0, 4.0)
    result = values * spread[None, :, None, None, None]
    return result.astype(jnp.bfloat16)


def level_of(rng, extent, shards, smallest, largest):
    level, own = 1.0, jax.random.fold_in(rng, 6)
    for dim, parts in shards:
        steps = jnp.exp(jax.random.uniform(jax.random.fold_in(own, dim), (parts,), jnp.float32, smallest / len(shards), largest / len(shards)))
        level = level * jnp.repeat(steps, extent[dim] // parts).reshape([-1 if axis == dim else 1 for axis in range(len(extent))])
    return level


def bell_draw(rng, extent, scale, most, split=(), kind=jnp.bfloat16):
    entries = jax.random.normal(rng, extent, jnp.float32) * scale
    if len(split) > 0:
        entries = level_of(rng, extent, split, -0.22, 0.18) * entries
    return jnp.clip(entries, min=-most, max=most).astype(kind)


def setup_inputs(seed: int = 0) -> dict:
    streams_of = jax.random.split(jax.random.key(seed), 6)
    coefficients = draw_coefficients(jax.random.fold_in(streams_of[5], 71), 0)
    section_factors = bell_draw(streams_of[1], (2, M, K, NB * K), K ** -0.5, 0.75, ((0, 2), (1, 64)))
    level_factors = bell_draw(streams_of[2], (2, LEVELS, M, K, NB * 2 * K), (2 * K) ** -0.5, 0.5, ((0, 2), (2, 64)))
    partners = draw_partners(jax.random.fold_in(streams_of[5], 71), 0)
    wave_ids = draw_wave_ids(jax.random.fold_in(streams_of[5], 71), 0)
    return dict(coefficients=coefficients, section_factors=section_factors, level_factors=level_factors, partners=partners, wave_ids=wave_ids)


def butterfly(coeff, section, levels, partners):
    count = coeff.shape[0]
    x = coeff.reshape(count, FIELDS, 2, NB, K).astype(jnp.float32)
    section_blocks = section.reshape(count, K, NB, K).astype(jnp.float32)
    z = jnp.einsum('sibj,sfrbj->sfrbi', section_blocks, x).astype(jnp.bfloat16)
    for level in range(LEVELS):
        across = z[:, :, :, partners[level]]
        factors = levels[level].reshape(count, K, NB, 2, K).astype(jnp.float32)
        summed = jnp.einsum('sibj,sfrbj->sfrbi', factors[:, :, :, 0], z.astype(jnp.float32))
        summed = summed + jnp.einsum('sibj,sfrbj->sfrbi', factors[:, :, :, 1], across.astype(jnp.float32))
        z = summed.astype(jnp.bfloat16)
    return z.reshape(count, FIELDS, 2, LATH)


def make_table(wave_ids, start, width):
    lon = start + jnp.arange(width, dtype=jnp.int32)
    phase = ((wave_ids[:, None] * lon[None, :]) % NLON).astype(jnp.float32) * (2.0 * math.pi / NLON)
    cosine = jnp.cos(phase)
    sine = jnp.sin(phase)
    waves = wave_ids.astype(jnp.float32)
    weight = jnp.where(wave_ids > 0, 2.0, 1.0).astype(jnp.float32)
    value = jnp.stack([weight[:, None] * cosine, -weight[:, None] * sine], axis=1)
    scaled = (weight * waves / M)[:, None]
    turned = jnp.stack([-scaled * sine, -scaled * cosine], axis=1)
    both = jnp.concatenate([value, turned], axis=2).reshape(M * 2, 2 * width)
    return both.astype(jnp.bfloat16)


def reference(coefficients, section_factors, level_factors, partners, wave_ids):
    group = M_DEV
    halves = []
    for parity in range(2):
        degree = wave_ids[:, None] + 2 * jnp.arange(LATH, dtype=jnp.int32)[None, :] + parity
        keep = (degree <= M - 1).astype(jnp.bfloat16)
        masked = coefficients[parity] * keep[:, None, None, :]

        def one_group(index):
            start = (index * group).astype(jnp.int32)
            coeff = lax.dynamic_slice_in_dim(masked, start, group, 0)
            section = lax.dynamic_slice_in_dim(section_factors[parity], start, group, 0)
            levels = lax.dynamic_slice_in_dim(level_factors[parity], start, group, 1)
            return butterfly(coeff, section, levels, partners)

        result = lax.map(one_group, jnp.arange(M // group, dtype=jnp.int32))
        halves.append(result.reshape(M, FIELDS, 2, LATH))
    evens = halves[0].astype(jnp.float32)
    odds = halves[1].astype(jnp.float32)
    spectra = jnp.stack([evens + odds, evens - odds]).astype(jnp.bfloat16)
    left = jnp.transpose(spectra, (0, 4, 2, 1, 3)).reshape(2 * LATH * FIELDS, M * 2)
    width = min(512, NLON)
    grid_parts = []
    slope_parts = []
    for start in range(0, NLON, width):
        table = make_table(wave_ids, start, width)
        product = jnp.dot(left, table, preferred_element_type=jnp.float32)
        grid_parts.append(product[:, :width].astype(jnp.bfloat16))
        slope_parts.append(product[:, width:].astype(jnp.bfloat16))
    grid = jnp.concatenate(grid_parts, axis=1).reshape(2, LATH, FIELDS, NLON)
    slope = jnp.concatenate(slope_parts, axis=1).reshape(2, LATH, FIELDS, NLON)
    return grid, slope
```

```python
import functools
import math

import jax
import jax.numpy as jnp
import numpy as np
from jax import lax
from jax.experimental import pallas as pl
from jax.experimental.pallas import tpu as pltpu
from jax.sharding import PartitionSpec as P

NLON = 4096
K = 64
NB = 16
NW = 16
NF = 10
M = 1024
LANES = 384
F32 = jnp.float32
BF16 = jnp.bfloat16
MESH = pl.DeviceIdType.MESH
NT = (((1,), (1,)), ((), ()))
TILE_WAVES = ((0, 6), (6, 12), (12, 16))


def target(g):
    return {"ma": g // 2, "ha": g % 2}


def xor_bits(a, b, bits):
    out = 0
    for i in range(bits):
        out = out + ((a // (1 << i) + b // (1 << i)) % 2) * (1 << i)
    return out


def iota(shape, dim):
    return lax.broadcasted_iota(jnp.int32, shape, dim)


def keep_waves(block, masks):
    return jnp.concatenate([jnp.where(m, block, jnp.zeros_like(block)) for m in masks], axis=0)


def synth_kernel(
    partners, waves, y_hbm, s_hbm, l_hbm, recv, yv, yf, zin, z0, z1, sv, lv, perm, send, in_sem, send_sem, recv_sem, own_sem
):
    ma = lax.axis_index("ma")
    ha = lax.axis_index("ha")
    me = ma * 2 + ha
    slot = ha * 64 + ma

    loads = [
        pltpu.make_async_copy(y_hbm, yv, in_sem.at[0]),
        pltpu.make_async_copy(s_hbm, sv, in_sem.at[1]),
        pltpu.make_async_copy(l_hbm.at[0], lv.at[0], in_sem.at[2]),
        pltpu.make_async_copy(l_hbm.at[1], lv.at[1], in_sem.at[3]),
    ]
    for load in loads:
        load.start()

    barrier = pltpu.get_barrier_semaphore()

    def greet(step, carry):
        g = (me + step) % 128
        pl.semaphore_signal(barrier, inc=1, device_id=target(g), device_id_type=MESH)
        return carry

    lax.fori_loop(1, 128, greet, 0)

    col = iota((1, LANES), 1)
    wave = col % 16
    fr = col // 16
    tile = (wave >= 6).astype(jnp.int32) + (wave >= 12).astype(jnp.int32)
    source = tile * 128 + (fr % 2) * 64 + (wave - 6 * tile) * 10 + fr // 2
    source = jnp.where(col < 320, source, -1)
    perm[...] = (iota((LANES, LANES), 0) == source).astype(F32).astype(BF16)
    eye = (iota((128, 128), 0) == iota((128, 128), 1)).astype(F32).astype(BF16)
    lane_wave = (iota((128, 128), 1) % 64) // 10
    masks = [lane_wave == w for w in range(6)]

    yf[pl.ds(2560, 512), :] = jnp.zeros((512, 128), F32)
    loads[0].wait()
    degree = 2 * ((iota((16, 128), 0) // 2) * 128 + iota((16, 128), 1)) + ha
    for w in range(NW):
        keep = degree <= (M - 1) - waves[ma * NW + w]
        for f in range(NF):
            row = (w * NF + f) * 16
            yf[pl.ds(row, 16), :] = jnp.where(keep, yv[pl.ds(row, 16), :].astype(F32), 0.0)
    for j in range(8):
        for t in range(3):
            rows = [yf[pl.ds(t * 960 + 2 * j + part, 64, stride=16), :] for part in range(2)]
            block = jnp.concatenate(rows, axis=0).astype(BF16)
            turned = lax.dot_general(eye, block, NT, preferred_element_type=F32)
            zin[j, :, pl.ds(t * 128, 128)] = turned.astype(BF16)

    loads[1].wait()
    low = iota((64, 128), 1) < 64

    def section(j, carry):
        lanes = pl.ds(pl.multiple_of(j * 128, 128), 128)
        for t, (first, last) in enumerate(TILE_WAVES):
            left = []
            for w in range(first, last):
                factor = sv[w, :, lanes]
                zero = jnp.zeros_like(factor)
                left.append(jnp.concatenate([jnp.where(low, factor, zero), jnp.where(low, zero, factor)], axis=0))
            right = keep_waves(zin[j, :, pl.ds(t * 128, 128)], masks[: last - first])
            out = jnp.dot(jnp.concatenate(left, axis=1), right, preferred_element_type=F32).astype(BF16)
            z0[2 * j, :, pl.ds(t * 128, 128)] = out[:64]
            z0[2 * j + 1, :, pl.ds(t * 128, 128)] = out[64:]
        return carry

    lax.fori_loop(0, 8, section, 0)

    def level(l, b, z):
        other = partners[l, b]
        lanes = pl.ds(pl.multiple_of(b * 128, 128), 128)
        outs = []
        for t, (first, last) in enumerate(TILE_WAVES):
            left = jnp.concatenate([lv[l, w, :, lanes] for w in range(first, last)], axis=1)
            both = jnp.concatenate([z[b, :, pl.ds(t * 128, 128)], z[other, :, pl.ds(t * 128, 128)]], axis=0)
            right = keep_waves(both, masks[: last - first])
            outs.append(jnp.dot(left, right, preferred_element_type=F32).astype(BF16))
        return outs

    loads[2].wait()

    def first_level(b, carry):
        for t, out in enumerate(level(0, b, z0)):
            z1[b, :, pl.ds(t * 128, 128)] = out
        return carry

    lax.fori_loop(0, NB, first_level, 0)
    loads[3].wait()
    pl.semaphore_wait(barrier, 127)

    own = pltpu.make_async_copy(send.at[me], recv.at[slot], own_sem)
    low_bits = [me % 2, (me // 2) % 2, (me // 4) % 2]

    def last_level(step, carry):
        b = xor_bits(me // 8, step, 4)
        state = jnp.concatenate(level(1, b, z1), axis=1)
        moved = jnp.dot(state, perm[...], preferred_element_type=F32)
        for t in range(3):
            send[pl.ds(b * 8, 8), t] = moved[:, t * 128 : (t + 1) * 128].reshape(8, 8, 128).astype(BF16)
        for r in range(8):
            g = b * 8
            for i in range(3):
                g = g + (1 - low_bits[i] if (r >> i) & 1 else low_bits[i]) * (1 << i)

            def go():
                pltpu.make_async_remote_copy(
                    send.at[g], recv.at[slot], send_sem, recv_sem, device_id=target(g), device_id_type=MESH
                ).start()

            if r == 0:
                pl.when(step > 0)(go)
                pl.when(step == 0)(own.start)
            else:
                go()
        return carry

    lax.fori_loop(0, NB, last_level, 0)
    own.wait()
    pltpu.make_async_remote_copy(
        send.at[pl.ds(0, 127)], recv.at[pl.ds(0, 127)], send_sem, recv_sem, device_id=target(me), device_id_type=MESH
    ).wait()


def synth(partners, waves, y, s, l):
    smem = pl.BlockSpec(memory_space=pltpu.SMEM)
    hbm = pl.BlockSpec(memory_space=pl.ANY)
    return pl.pallas_call(
        synth_kernel,
        out_shape=jax.ShapeDtypeStruct((128, 3, 8, 128), BF16),
        in_specs=[smem, smem, hbm, hbm, hbm],
        out_specs=hbm,
        scratch_shapes=[
            pltpu.VMEM((2560, 128), BF16),
            pltpu.VMEM((3072, 128), F32),
            pltpu.VMEM((8, 128, LANES), BF16),
            pltpu.VMEM((NB, K, LANES), BF16),
            pltpu.VMEM((NB, K, LANES), BF16),
            pltpu.VMEM((NW, K, 1024), BF16),
            pltpu.VMEM((2, NW, K, 2048), BF16),
            pltpu.VMEM((LANES, LANES), BF16),
            pltpu.VMEM((128, 3, 8, 128), BF16),
            pltpu.SemaphoreType.DMA((4,)),
            pltpu.SemaphoreType.DMA,
            pltpu.SemaphoreType.DMA,
            pltpu.SemaphoreType.DMA,
        ],
        compiler_params=pltpu.CompilerParams(collective_id=0, has_side_effects=True, vmem_limit_bytes=40 << 20),
    )(partners, waves, y, s, l)


def dft_tables():
    a = np.arange(128)
    out = np.zeros((4, 8, 256, 256), np.float64)
    for c in range(4):
        lon = 128 * c + np.arange(128)
        for b in range(8):
            angle = 2.0 * math.pi * (((8 * a + b)[:, None] * lon[None, :]) % NLON) / NLON
            cos, sin = np.cos(angle), np.sin(angle)
            out[c, b] = np.block([[cos, sin], [-sin, cos]])
    return out.astype(np.float32)


def grid_kernel(recv, waves, table_hbm, grid_hbm, slope_hbm, wf, left, table, g, out, in_sem, out_sem):
    load = pltpu.make_async_copy(table_hbm, table, in_sem)
    load.start()
    group = iota((8, 128), 1) // 16

    def spread(j, carry):
        lanes = pl.ds(pl.multiple_of(j * 128, 128), 128)
        for q in range(3):
            sides = []
            for p in range(2):
                rows = [recv[p * 64 + 8 * j + i, q].astype(F32) for i in range(8)]
                for d in (4, 2, 1):
                    upper = (group // d) % 2 == 1
                    new = list(rows)
                    for i in range(len(rows)):
                        if i & d or i + d >= len(rows):
                            continue
                        one, two = rows[i], rows[i + d]
                        new[i] = jnp.where(upper, pltpu.roll(two, 16 * d, 1), one)
                        new[i + d] = jnp.where(upper, two, pltpu.roll(one, 128 - 16 * d, 1))
                    rows = new
                    if q == 2 and d == 4:
                        rows = rows[:4]
                sides.append(rows)
            for i in range(len(sides[0])):
                fr = q * 8 + i
                even, odd = sides[0][i], sides[1][i]
                row = (fr % 2) * 160 + (fr // 2) * 8
                wf[pl.ds(row, 8), lanes] = even + odd
                wf[pl.ds(row + 80, 8), lanes] = even - odd
        return carry

    lax.fori_loop(0, 8, spread, 0)

    spectra = wf[...].astype(BF16)
    slot_wave = waves[...]
    for b in range(8):
        k = 8 * iota((128, 1), 0) + b
        weight = jnp.where(k > 0, 2.0, 1.0)
        pick = jnp.where(slot_wave == k, weight, 0.0).astype(BF16)
        moved = lax.dot_general(spectra, pick, NT, preferred_element_type=F32)
        real, imag = moved[:160], moved[160:]
        scale = (8 * iota((1, 128), 1) + b).astype(F32) * (1.0 / M)
        left[b, pl.ds(0, 160), pl.ds(0, 128)] = real.astype(BF16)
        left[b, pl.ds(0, 160), pl.ds(128, 128)] = imag.astype(BF16)
        left[b, pl.ds(160, 160), pl.ds(0, 128)] = (-scale * imag).astype(BF16)
        left[b, pl.ds(160, 160), pl.ds(128, 128)] = (scale * real).astype(BF16)

    load.wait()
    root = math.sqrt(0.5)
    copies = []
    for c in range(4):
        for b in range(8):
            g[b] = jnp.dot(left[b], table[c, b], preferred_element_type=F32)

        def combine(i, carry, c=c):
            rows = pl.ds(pl.multiple_of(i * 16, 16), 16)
            re = [g[b, rows, pl.ds(0, 128)] for b in range(8)]
            im = [None if b in (0, 4) else g[b, rows, pl.ds(128, 128)] for b in range(8)]
            plus, minus = re[0] + re[4], re[0] - re[4]
            r26, i26 = re[2] + re[6], im[6] - im[2]
            even = [plus + r26, minus + i26, plus - r26, minus - i26]
            r17, r35 = re[1] + re[7], re[3] + re[5]
            i71, i53 = im[7] - im[1], im[5] - im[3]
            rr, ii = root * (r17 - r35), root * (i71 + i53)
            odd = [r17 + r35, ii + rr, i71 - i53, ii - rr]
            for j in range(4):
                out[rows, pl.ds(512 * j + 128 * c, 128)] = (even[j] + odd[j]).astype(BF16)
                out[rows, pl.ds(512 * j + 2048 + 128 * c, 128)] = (even[j] - odd[j]).astype(BF16)
            return carry

        lax.fori_loop(0, 20, combine, 0)
        for j in range(8):
            lanes = pl.ds(512 * j + 128 * c, 128)
            for n, target_hbm in enumerate((grid_hbm, slope_hbm)):
                copy = pltpu.make_async_copy(out.at[pl.ds(160 * n, 160), lanes], target_hbm.at[:, lanes], out_sem.at[len(copies)])
                copy.start()
                copies.append(copy)
    for copy in copies:
        copy.wait()


def to_grid(recv, waves, table):
    vmem = pl.BlockSpec(memory_space=pltpu.VMEM)
    hbm = pl.BlockSpec(memory_space=pl.ANY)
    shape = jax.ShapeDtypeStruct((160, NLON), BF16)
    return pl.pallas_call(
        grid_kernel,
        out_shape=(shape, shape),
        in_specs=[vmem, vmem, hbm],
        out_specs=(hbm, hbm),
        scratch_shapes=[
            pltpu.VMEM((320, 1024), F32),
            pltpu.VMEM((8, 320, 256), BF16),
            pltpu.VMEM((4, 8, 256, 256), BF16),
            pltpu.VMEM((8, 320, 256), F32),
            pltpu.VMEM((320, NLON), BF16),
            pltpu.SemaphoreType.DMA,
            pltpu.SemaphoreType.DMA((64,)),
        ],
        compiler_params=pltpu.CompilerParams(vmem_limit_bytes=40 << 20),
    )(recv, waves, table)


def body(coefficients, section_factors, level_factors, partners, wave_ids):
    y = coefficients.reshape(NW * NF, 2, 2, 4, 128).transpose(0, 2, 3, 1, 4).reshape(NW * NF * 16, 128)
    recv = synth(partners, wave_ids, y, section_factors[0], level_factors[0])
    grid, slope = to_grid(recv, wave_ids.reshape(1, M), jnp.asarray(dft_tables(), BF16))
    shape = (2, NF, 8, NLON)
    return (
        grid.reshape(shape).transpose(0, 2, 1, 3),
        slope.reshape(shape).transpose(0, 2, 1, 3),
    )


def solution(mesh):
    in_specs = (
        P("ha", "ma", None, None, None),
        P("ha", "ma", None, None),
        P("ha", None, "ma", None, None),
        P(),
        P(),
    )
    out_specs = (P(None, ("ma", "ha"), None, None), P(None, ("ma", "ha"), None, None))
    return jax.shard_map(body, mesh=mesh, in_specs=in_specs, out_specs=out_specs, check_vma=False)
```

```python
import functools
import math

import jax
import jax.numpy as jnp
import numpy as np
from jax import lax
from jax.experimental import pallas as pl
from jax.experimental.pallas import tpu as pltpu
from jax.sharding import PartitionSpec as P

NLON = 4096
K = 64
NB = 16
NW = 16
NF = 10
M = 1024
LANES = 384
F32 = jnp.float32
BF16 = jnp.bfloat16
MESH = pl.DeviceIdType.MESH
NT = (((1,), (1,)), ((), ()))
TILE_WAVES = ((0, 6), (6, 12), (12, 16))


def target(g):
    return {"ma": g // 2, "ha": g % 2}


def iota(shape, dim):
    return lax.broadcasted_iota(jnp.int32, shape, dim)


def keep_waves(block, masks):
    return jnp.concatenate([jnp.where(m, block, jnp.zeros_like(block)) for m in masks], axis=0)


ORDER = (5, 3, 7, 4, 1, 2, 6, 0)


def pick(bit, base):
    return 1 - base if bit else base


def synth_kernel(
    partners_hbm, waves_hbm, table_hbm, y_hbm, s_hbm, l_hbm, left,
    partners, waves, wave_rows, yv, yf, zin, z0, z1, sv, lv, perm, send, recv, acc, in_sem, send_sem, recv_sem, own_sem,
):
    ma = lax.axis_index("ma")
    ha = lax.axis_index("ha")
    me = ma * 2 + ha
    slot = ha * 64 + ma

    loads = [
        pltpu.make_async_copy(y_hbm, yv, in_sem.at[0]),
        pltpu.make_async_copy(waves_hbm, waves, in_sem.at[1]),
        pltpu.make_async_copy(partners_hbm, partners, in_sem.at[2]),
        pltpu.make_async_copy(table_hbm, wave_rows, in_sem.at[3]),
        pltpu.make_async_copy(s_hbm, sv, in_sem.at[4]),
        pltpu.make_async_copy(l_hbm.at[0], lv.at[0], in_sem.at[5]),
        pltpu.make_async_copy(l_hbm.at[1], lv.at[1], in_sem.at[6]),
    ]
    for load in loads[:6]:
        load.start()

    barrier = pltpu.get_barrier_semaphore()

    def greet(first, last):
        for step in range(max(first, 1), last):
            pl.semaphore_signal(barrier, inc=1, device_id=target((me + step) % 128), device_id_type=MESH)

    col = iota((1, LANES), 1)
    col = jnp.where(col < 320, col, col - 64)
    wave = col % 16
    fr = col // 16
    tile = (wave >= 6).astype(jnp.int32) + (wave >= 12).astype(jnp.int32)
    source = tile * 128 + (fr % 2) * 64 + (wave - 6 * tile) * 10 + fr // 2
    perm[...] = (iota((LANES, LANES), 0) == source).astype(F32).astype(BF16)
    eye = (iota((128, 128), 0) == iota((128, 128), 1)).astype(F32).astype(BF16)
    lane_wave = (iota((128, 128), 1) % 64) // 10
    masks = [lane_wave == w for w in range(6)]

    yf[pl.ds(2560, 512), :] = jnp.zeros((512, 128), F32)
    degree = 2 * ((iota((16, 128), 0) // 2) * 128 + iota((16, 128), 1)) + ha
    greet(0, 16)
    loads[1].wait()
    loads[0].wait()
    for w in range(NW):
        keep = degree <= (M - 1) - waves[ma * NW + w]
        for f in range(NF):
            row = (w * NF + f) * 16
            yf[pl.ds(row, 16), :] = jnp.where(keep, yv[pl.ds(row, 16), :].astype(F32), 0.0)
        greet(16 + 7 * w, 23 + 7 * w)
    for j in range(8):
        for t in range(3):
            rows = [yf[pl.ds(t * 960 + 2 * j + part, 64, stride=16), :] for part in range(2)]
            block = jnp.concatenate(rows, axis=0).astype(BF16)
            turned = lax.dot_general(eye, block, NT, preferred_element_type=F32)
            zin[j, :, pl.ds(t * 128, 128)] = turned.astype(BF16)

    loads[4].wait()
    loads[6].start()
    low = iota((64, 128), 1) < 64

    def section(j, carry):
        lanes = pl.ds(pl.multiple_of(j * 128, 128), 128)
        for t, (first, last) in enumerate(TILE_WAVES):
            halves = []
            for w in range(first, last):
                factor = sv[w, :, lanes]
                zero = jnp.zeros_like(factor)
                halves.append(jnp.concatenate([jnp.where(low, factor, zero), jnp.where(low, zero, factor)], axis=0))
            right = keep_waves(zin[j, :, pl.ds(t * 128, 128)], masks[: last - first])
            out = jnp.dot(jnp.concatenate(halves, axis=1), right, preferred_element_type=F32).astype(BF16)
            z0[2 * j, :, pl.ds(t * 128, 128)] = out[:64]
            z0[2 * j + 1, :, pl.ds(t * 128, 128)] = out[64:]
        return carry

    lax.fori_loop(0, 8, section, 0, unroll=2)

    def level(l, b, z):
        other = partners[l, b]
        lanes = pl.ds(pl.multiple_of(b * 128, 128), 128)
        outs = []
        for t, (first, last) in enumerate(TILE_WAVES):
            factors = jnp.concatenate([lv[l, w, :, lanes] for w in range(first, last)], axis=1)
            both = jnp.concatenate([z[b, :, pl.ds(t * 128, 128)], z[other, :, pl.ds(t * 128, 128)]], axis=0)
            right = keep_waves(both, masks[: last - first])
            outs.append(jnp.dot(factors, right, preferred_element_type=F32).astype(BF16))
        return outs

    loads[2].wait()
    loads[3].wait()
    loads[5].wait()

    def first_level(b, carry):
        for t, out in enumerate(level(0, b, z0)):
            z1[b, :, pl.ds(t * 128, 128)] = out
        return carry

    lax.fori_loop(0, NB, first_level, 0, unroll=4)
    loads[6].wait()
    pl.semaphore_wait(barrier, 127)

    own = pltpu.make_async_copy(send.at[me], recv.at[slot], own_sem)
    pair = me // 16
    low_bits = [me % 2, (me // 2) % 2, (me // 4) % 2, (me // 8) % 2]
    high = [pair % 2, (pair // 2) % 2, pair // 4]
    half = iota((16, 4, 128), 2) < 64

    def partner_pair(mask):
        return sum(pick((mask >> i) & 1, high[i]) * (1 << i) for i in range(3))

    for i, mask in enumerate(ORDER):
        p = partner_pair(mask)
        blocks = [level(1, 2 * p + k, z1) for k in range(2)]
        state = jnp.concatenate([jnp.concatenate(outs, axis=1) for outs in blocks], axis=0)
        moved = jnp.dot(state, perm[...], preferred_element_type=F32)
        groups = pl.ds(p * 16, 16)
        for t in range(3):
            rows = moved[:, t * 128 : (t + 1) * 128].reshape(16, 8, 128)
            if t < 2:
                send[groups, 2 * t] = rows[:, :4].astype(BF16)
                send[groups, 2 * t + 1] = rows[:, 4:].astype(BF16)
            else:
                send[groups, 4] = jnp.where(half, rows[:, :4], rows[:, 4:]).astype(BF16)
        for r in range(15, -1, -1):
            g = p * 16 + sum(pick((r >> n) & 1, low_bits[n]) * (1 << n) for n in range(4))
            if mask == 0 and r == 0:
                own.start()
            else:
                pltpu.make_async_remote_copy(
                    send.at[g], recv.at[slot], send_sem, recv_sem.at[i], device_id=target(g), device_id_type=MESH
                ).start()

    group = iota((8, 128), 1) // 16
    for i, mask in enumerate(ORDER):
        j = partner_pair(mask)
        slot_wave = wave_rows[pl.ds(j, 1), :]
        row = iota((M, 1), 0)
        k = 8 * (row % 128) + row // 128
        weight = jnp.where(k > 0, 2.0, 1.0)
        onehot = jnp.where(slot_wave == k, weight, 0.0).astype(BF16)
        count = 16 if mask else 15
        pltpu.make_async_remote_copy(
            send.at[pl.ds(0, count)], recv.at[pl.ds(0, count)], send_sem, recv_sem.at[i],
            device_id=target(me), device_id_type=MESH,
        ).wait_recv()
        if mask == 0:
            own.wait()
        parts = [[None] * 20, [None] * 20]
        for q in range(3):
            sides = []
            for p in range(2):
                rows = []
                for n in range(8):
                    message = recv.at[p * 64 + 8 * j + n]
                    if q < 2:
                        rows.append(jnp.concatenate([message[2 * q].astype(F32), message[2 * q + 1].astype(F32)], axis=0))
                    else:
                        packed = message[4].astype(F32)
                        both = jnp.concatenate([packed, packed], axis=0)
                        rows.append(jnp.where(iota((8, 128), 0) < 4, both, pltpu.roll(both, 64, 1)))
                for d in (4, 2, 1):
                    upper = (group // d) % 2 == 1
                    new = list(rows)
                    for n in range(len(rows)):
                        if n & d or n + d >= len(rows):
                            continue
                        one, two = rows[n], rows[n + d]
                        new[n] = jnp.where(upper, pltpu.roll(two, 16 * d, 1), one)
                        new[n + d] = jnp.where(upper, two, pltpu.roll(one, 128 - 16 * d, 1))
                    rows = new
                    if q == 2 and d == 4:
                        rows = rows[:4]
                sides.append(rows)
            for n, (even, odd) in enumerate(zip(*sides)):
                fr = q * 8 + n
                parts[fr % 2][fr // 2] = even + odd
                parts[fr % 2][10 + fr // 2] = even - odd
        spectra = jnp.concatenate(parts[0] + parts[1], axis=0).astype(BF16)
        for b in range(8):
            lanes = pl.ds(b * 128, 128)
            moved = lax.dot_general(spectra, onehot[b * 128 : (b + 1) * 128], NT, preferred_element_type=F32)
            if i > 0:
                moved = moved + acc[:, lanes]
            if i < 7:
                acc[:, lanes] = moved
            else:
                real, imag = moved[:160], moved[160:]
                scale = (8 * iota((1, 128), 1) + b).astype(F32) * (1.0 / M)
                left[b, pl.ds(0, 160), pl.ds(0, 128)] = real.astype(BF16)
                left[b, pl.ds(0, 160), pl.ds(128, 128)] = imag.astype(BF16)
                left[b, pl.ds(160, 160), pl.ds(0, 128)] = (-scale * imag).astype(BF16)
                left[b, pl.ds(160, 160), pl.ds(128, 128)] = (scale * real).astype(BF16)

    pltpu.make_async_remote_copy(
        send.at[pl.ds(0, 127)], recv.at[pl.ds(0, 127)], send_sem, recv_sem.at[0], device_id=target(me), device_id_type=MESH
    ).wait_send()


def synth(partners, waves, y, s, l):
    hbm = pl.BlockSpec(memory_space=pltpu.HBM)
    return pl.pallas_call(
        synth_kernel,
        out_shape=jax.ShapeDtypeStruct((8, 320, 256), BF16),
        in_specs=[hbm] * 6,
        out_specs=pl.BlockSpec(memory_space=pltpu.VMEM),
        scratch_shapes=[
            pltpu.SMEM((2, NB), jnp.int32),
            pltpu.SMEM((M,), jnp.int32),
            pltpu.VMEM((8, 128), jnp.int32),
            pltpu.VMEM((2560, 128), BF16),
            pltpu.VMEM((3072, 128), F32),
            pltpu.VMEM((8, 128, LANES), BF16),
            pltpu.VMEM((NB, K, LANES), BF16),
            pltpu.VMEM((NB, K, LANES), BF16),
            pltpu.VMEM((NW, K, 1024), BF16),
            pltpu.VMEM((2, NW, K, 2048), BF16),
            pltpu.VMEM((LANES, LANES), BF16),
            pltpu.VMEM((128, 5, 4, 128), BF16),
            pltpu.VMEM((128, 5, 4, 128), BF16),
            pltpu.VMEM((320, M), F32),
            pltpu.SemaphoreType.DMA((7,)),
            pltpu.SemaphoreType.DMA,
            pltpu.SemaphoreType.DMA((8,)),
            pltpu.SemaphoreType.DMA,
        ],
        compiler_params=pltpu.CompilerParams(collective_id=0, has_side_effects=True, vmem_limit_bytes=32 << 20),
    )(*[pltpu.with_memory_space_constraint(v, pltpu.HBM) for v in (partners, waves, waves.reshape(8, 128), y, s, l)])


def dft_tables():
    a, lon = np.arange(128), np.arange(512)
    out = np.zeros((8, 256, 1024), np.float64)
    for b in range(8):
        angle = 2.0 * math.pi * (((8 * a + b)[:, None] * lon[None, :]) % NLON) / NLON
        cos, sin = np.cos(angle), np.sin(angle)
        out[b] = np.block([[cos, sin], [-sin, cos]])
    return out.astype(np.float32)


def grid_kernel(left, table, grid_hbm, slope_hbm, g, out, out_sem):
    for b in range(8):
        if b in (0, 4):
            g[b, :, pl.ds(0, 512)] = jnp.dot(left[b], table[b, :, pl.ds(0, 512)], preferred_element_type=F32)
        else:
            g[b] = jnp.dot(left[b], table[b], preferred_element_type=F32)

    root = math.sqrt(0.5)
    for n, target_hbm in enumerate((grid_hbm, slope_hbm)):

        def combine(i, carry, n=n, target_hbm=target_hbm):
            rows = pl.ds(pl.multiple_of(n * 160 + i * 16, 16), 16)
            for c in range(4):
                re = [g[b, rows, pl.ds(128 * c, 128)] for b in range(8)]
                im = [None if b in (0, 4) else g[b, rows, pl.ds(512 + 128 * c, 128)] for b in range(8)]
                plus, minus = re[0] + re[4], re[0] - re[4]
                r26, i26 = re[2] + re[6], im[6] - im[2]
                even = [plus + r26, minus + i26, plus - r26, minus - i26]
                r17, r35 = re[1] + re[7], re[3] + re[5]
                i71, i53 = im[7] - im[1], im[5] - im[3]
                rr, ii = root * (r17 - r35), root * (i71 + i53)
                odd = [r17 + r35, ii + rr, i71 - i53, ii - rr]
                for j in range(4):
                    out[rows, pl.ds(512 * j + 128 * c, 128)] = (even[j] + odd[j]).astype(BF16)
                    out[rows, pl.ds(512 * j + 2048 + 128 * c, 128)] = (even[j] - odd[j]).astype(BF16)
            pltpu.make_async_copy(out.at[rows], target_hbm.at[pl.ds(pl.multiple_of(i * 16, 16), 16)], out_sem.at[n]).start()
            return carry

        lax.fori_loop(0, 10, combine, 0)
    for n, target_hbm in enumerate((grid_hbm, slope_hbm)):
        pltpu.make_async_copy(out.at[pl.ds(160 * n, 160)], target_hbm, out_sem.at[n]).wait()


def to_grid(left, table):
    vmem = pl.BlockSpec(memory_space=pltpu.VMEM)
    hbm = pl.BlockSpec(memory_space=pltpu.HBM)
    shape = jax.ShapeDtypeStruct((160, NLON), BF16)
    return pl.pallas_call(
        grid_kernel,
        out_shape=(shape, shape),
        in_specs=[vmem, vmem],
        out_specs=(hbm, hbm),
        scratch_shapes=[
            pltpu.VMEM((8, 320, 1024), F32),
            pltpu.VMEM((320, NLON), BF16),
            pltpu.SemaphoreType.DMA((2,)),
        ],
        compiler_params=pltpu.CompilerParams(vmem_limit_bytes=32 << 20),
    )(left, table)


def body(coefficients, section_factors, level_factors, partners, wave_ids):
    y = coefficients.reshape(NW * NF, 2, 2, 4, 128).transpose(0, 2, 3, 1, 4).reshape(NW * NF * 16, 128)
    left = synth(partners, wave_ids, y, section_factors[0], level_factors[0])
    grid, slope = to_grid(left, jnp.asarray(dft_tables(), BF16))
    shape = (2, NF, 8, NLON)
    return (
        grid.reshape(shape).transpose(0, 2, 1, 3),
        slope.reshape(shape).transpose(0, 2, 1, 3),
    )


def solution(mesh):
    in_specs = (
        P("ha", "ma", None, None, None),
        P("ha", "ma", None, None),
        P("ha", None, "ma", None, None),
        P(),
        P(),
    )
    out_specs = (P(None, ("ma", "ha"), None, None), P(None, ("ma", "ha"), None, None))
    return jax.shard_map(body, mesh=mesh, in_specs=in_specs, out_specs=out_specs, check_vma=False)
```

```python
import functools
import math

import jax
import jax.numpy as jnp
import numpy as np
from jax import lax
from jax.experimental import pallas as pl
from jax.experimental.pallas import tpu as pltpu
from jax.sharding import PartitionSpec as P

NLON = 4096
K = 64
NB = 16
NW = 16
NF = 10
M = 1024
LANES = 384
F32 = jnp.float32
BF16 = jnp.bfloat16
MESH = pl.DeviceIdType.MESH
NT = (((1,), (1,)), ((), ()))
TILE_WAVES = ((0, 6), (6, 12), (12, 16))


def target(g):
    return {"ma": g // 2, "ha": g % 2}


def iota(shape, dim):
    return lax.broadcasted_iota(jnp.int32, shape, dim)


def keep_waves(block, masks):
    return jnp.concatenate([jnp.where(m, block, jnp.zeros_like(block)) for m in masks], axis=0)


ORDER = (7, 3, 5, 1, 6, 2, 4, 0)


def pick(bit, base):
    return 1 - base if bit else base


def mask_at(step, place):
    return ORDER[(step + 2 * place) % 8]


def synth_kernel(
    partners_hbm, waves_hbm, table_hbm, y_hbm, s_hbm, l_hbm, left,
    partners, waves, wave_rows, yv, yf, zin, z0, z1, sv, lv, perm, send, recv, acc, in_sem, send_sem, recv_sem,
):
    ma = lax.axis_index("ma")
    ha = lax.axis_index("ha")
    me = ma * 2 + ha
    slot = ha * 64 + ma

    loads = [
        pltpu.make_async_copy(y_hbm, yv, in_sem.at[0]),
        pltpu.make_async_copy(waves_hbm, waves, in_sem.at[1]),
        pltpu.make_async_copy(partners_hbm, partners, in_sem.at[2]),
        pltpu.make_async_copy(table_hbm, wave_rows, in_sem.at[3]),
        pltpu.make_async_copy(s_hbm, sv, in_sem.at[4]),
        pltpu.make_async_copy(l_hbm.at[0], lv.at[0], in_sem.at[5]),
        pltpu.make_async_copy(l_hbm.at[1], lv.at[1], in_sem.at[6]),
    ]
    for load in loads[:6]:
        load.start()

    barrier = pltpu.get_barrier_semaphore()

    def greet(first, last):
        for step in range(max(first, 1), last):
            pl.semaphore_signal(barrier, inc=1, device_id=target((me + step) % 128), device_id_type=MESH)

    col = iota((1, LANES), 1)
    col = jnp.where(col < 320, col, col - 64)
    wave = col % 16
    fr = col // 16
    tile = (wave >= 6).astype(jnp.int32) + (wave >= 12).astype(jnp.int32)
    source = tile * 128 + (fr % 2) * 64 + (wave - 6 * tile) * 10 + fr // 2
    perm[...] = (iota((LANES, LANES), 0) == source).astype(F32).astype(BF16)
    eye = (iota((128, 128), 0) == iota((128, 128), 1)).astype(F32).astype(BF16)
    lane_wave = (iota((128, 128), 1) % 64) // 10
    masks = [lane_wave == w for w in range(6)]

    yf[pl.ds(3840, 768), :] = jnp.zeros((768, 128), F32)
    degree = 2 * ((iota((16, 128), 0) // 2) * 128 + iota((16, 128), 1)) + ha
    greet(0, 64)
    loads[1].wait()
    loads[0].wait()
    for w in range(NW):
        keep = degree <= (M - 1) - waves[ma * NW + w]
        for f in range(NF):
            row = (w * NF + f) * 16
            yf[pl.ds((w * NF + f) * 24, 16), :] = jnp.where(keep, yv[pl.ds(row, 16), :].astype(F32), 0.0)
        greet(64 + 4 * w, 68 + 4 * w)
    for j in range(8):
        for t in range(3):
            rows = [yf[pl.ds(t * 1440 + 2 * j + part, 64, stride=24), :] for part in range(2)]
            block = jnp.concatenate(rows, axis=0).astype(BF16)
            turned = lax.dot_general(eye, block, NT, preferred_element_type=F32)
            zin[j, :, pl.ds(t * 128, 128)] = turned.astype(BF16)

    loads[4].wait()
    loads[6].start()
    low = iota((64, 128), 1) < 64

    def section(j, carry):
        lanes = pl.ds(pl.multiple_of(j * 128, 128), 128)
        for t, (first, last) in enumerate(TILE_WAVES):
            halves = []
            for w in range(first, last):
                factor = sv[w, :, lanes]
                zero = jnp.zeros_like(factor)
                halves.append(jnp.concatenate([jnp.where(low, factor, zero), jnp.where(low, zero, factor)], axis=0))
            right = keep_waves(zin[j, :, pl.ds(t * 128, 128)], masks[: last - first])
            out = jnp.dot(jnp.concatenate(halves, axis=1), right, preferred_element_type=F32).astype(BF16)
            z0[2 * j, :, pl.ds(t * 128, 128)] = out[:64]
            z0[2 * j + 1, :, pl.ds(t * 128, 128)] = out[64:]
        return carry

    lax.fori_loop(0, 8, section, 0, unroll=2)

    def level(l, b, z):
        other = partners[l, b]
        lanes = pl.ds(pl.multiple_of(b * 128, 128), 128)
        outs = []
        for t, (first, last) in enumerate(TILE_WAVES):
            factors = jnp.concatenate([lv[l, w, :, lanes] for w in range(first, last)], axis=1)
            both = jnp.concatenate([z[b, :, pl.ds(t * 128, 128)], z[other, :, pl.ds(t * 128, 128)]], axis=0)
            right = keep_waves(both, masks[: last - first])
            outs.append(jnp.dot(factors, right, preferred_element_type=F32).astype(BF16))
        return outs

    loads[2].wait()
    loads[3].wait()
    loads[5].wait()

    def first_level(b, carry):
        for t, out in enumerate(level(0, b, z0)):
            z1[b, :, pl.ds(t * 128, 128)] = out
        return carry

    lax.fori_loop(0, NB, first_level, 0, unroll=4)
    loads[6].wait()
    pl.semaphore_wait(barrier, 127)

    pair = me // 16
    low_bits = [me % 2, (me // 2) % 2, (me // 4) % 2, (me // 8) % 2]
    high = [pair % 2, (pair // 2) % 2, pair // 4]
    half = iota((16, 4, 128), 2) < 64

    at_place = [pick(1 - (n & 1), low_bits[1]) * pick(1 - (n >> 1), low_bits[2]) for n in range(4)]

    def partner_pair(mask):
        return sum(pick((mask >> i) & 1, high[i]) * (1 << i) for i in range(3))

    for i in range(8):
        p = sum(at_place[n] * partner_pair(mask_at(i, n)) for n in range(4))
        own = p == pair
        blocks = [level(1, 2 * p + k, z1) for k in range(2)]
        state = jnp.concatenate([jnp.concatenate(outs, axis=1) for outs in blocks], axis=0)
        moved = jnp.dot(state, perm[...], preferred_element_type=F32)
        groups = pl.ds(p * 16, 16)
        for t in range(3):
            rows = moved[:, t * 128 : (t + 1) * 128].reshape(16, 8, 128)
            if t < 2:
                send[groups, 2 * t] = rows[:, :4].astype(BF16)
                send[groups, 2 * t + 1] = rows[:, 4:].astype(BF16)
            else:
                send[groups, 4] = jnp.where(half, rows[:, :4], rows[:, 4:]).astype(BF16)
        for r in range(15, -1, -1):
            g = p * 16 + sum(pick((r >> n) & 1, low_bits[n]) * (1 << n) for n in range(4))

            def go():
                pltpu.make_async_remote_copy(
                    send.at[g], recv.at[slot], send_sem, recv_sem.at[i], device_id=target(g), device_id_type=MESH
                ).start()

            if r == 0:
                pl.when(jnp.logical_not(own))(go)
                pl.when(own)(pltpu.make_async_copy(send.at[g], recv.at[slot], recv_sem.at[i]).start)
            else:
                go()

    group = iota((8, 128), 1) // 16
    lane_place = (iota((1, 128), 1) // 16) % 4
    for i in range(8):
        pairs = [partner_pair(mask_at(i, n)) for n in range(4)]
        slot_wave = wave_rows[pl.ds(pairs[0], 1), :]
        for n in range(1, 4):
            slot_wave = jnp.where(lane_place == n, wave_rows[pl.ds(pairs[n], 1), :], slot_wave)
        row = iota((M, 1), 0)
        k = 8 * (row % 128) + row // 128
        weight = jnp.where(k > 0, 2.0, 1.0)
        onehot = jnp.where(slot_wave == k, weight, 0.0).astype(BF16)
        pltpu.make_async_remote_copy(
            send.at[pl.ds(0, 16)], recv.at[pl.ds(0, 16)], send_sem, recv_sem.at[i],
            device_id=target(me), device_id_type=MESH,
        ).wait_recv()
        parts = [[None] * 20, [None] * 20]
        for q in range(3):
            sides = []
            for p in range(2):
                rows = []
                for n in range(8):
                    message = recv.at[p * 64 + 8 * pairs[n % 4] + n]
                    if q < 2:
                        rows.append(jnp.concatenate([message[2 * q].astype(F32), message[2 * q + 1].astype(F32)], axis=0))
                    else:
                        packed = message[4].astype(F32)
                        both = jnp.concatenate([packed, packed], axis=0)
                        rows.append(jnp.where(iota((8, 128), 0) < 4, both, pltpu.roll(both, 64, 1)))
                for d in (4, 2, 1):
                    upper = (group // d) % 2 == 1
                    new = list(rows)
                    for n in range(len(rows)):
                        if n & d or n + d >= len(rows):
                            continue
                        one, two = rows[n], rows[n + d]
                        new[n] = jnp.where(upper, pltpu.roll(two, 16 * d, 1), one)
                        new[n + d] = jnp.where(upper, two, pltpu.roll(one, 128 - 16 * d, 1))
                    rows = new
                    if q == 2 and d == 4:
                        rows = rows[:4]
                sides.append(rows)
            for n, (even, odd) in enumerate(zip(*sides)):
                fr = q * 8 + n
                parts[fr % 2][fr // 2] = even + odd
                parts[fr % 2][10 + fr // 2] = even - odd
        spectra = jnp.concatenate(parts[0] + parts[1], axis=0).astype(BF16)
        for b in range(8):
            lanes = pl.ds(b * 128, 128)
            moved = lax.dot_general(spectra, onehot[b * 128 : (b + 1) * 128], NT, preferred_element_type=F32)
            if i > 0:
                moved = moved + acc[:, lanes]
            if i < 7:
                acc[:, lanes] = moved
            else:
                real, imag = moved[:160], moved[160:]
                scale = (8 * iota((1, 128), 1) + b).astype(F32) * (1.0 / M)
                left[b, pl.ds(0, 160), pl.ds(0, 128)] = real.astype(BF16)
                left[b, pl.ds(0, 160), pl.ds(128, 128)] = imag.astype(BF16)
                left[b, pl.ds(160, 160), pl.ds(0, 128)] = (-scale * imag).astype(BF16)
                left[b, pl.ds(160, 160), pl.ds(128, 128)] = (scale * real).astype(BF16)

    pltpu.make_async_remote_copy(
        send.at[pl.ds(0, 127)], recv.at[pl.ds(0, 127)], send_sem, recv_sem.at[0], device_id=target(me), device_id_type=MESH
    ).wait_send()


def synth(partners, waves, y, s, l):
    hbm = pl.BlockSpec(memory_space=pltpu.HBM)
    return pl.pallas_call(
        synth_kernel,
        out_shape=jax.ShapeDtypeStruct((8, 320, 256), BF16),
        in_specs=[hbm] * 6,
        out_specs=pl.BlockSpec(memory_space=pltpu.VMEM),
        scratch_shapes=[
            pltpu.SMEM((2, NB), jnp.int32),
            pltpu.SMEM((M,), jnp.int32),
            pltpu.VMEM((8, 128), jnp.int32),
            pltpu.VMEM((2560, 128), BF16),
            pltpu.VMEM((4608, 128), F32),
            pltpu.VMEM((8, 128, LANES), BF16),
            pltpu.VMEM((NB, K, LANES), BF16),
            pltpu.VMEM((NB, K, LANES), BF16),
            pltpu.VMEM((NW, K, 1024), BF16),
            pltpu.VMEM((2, NW, K, 2048), BF16),
            pltpu.VMEM((LANES, LANES), BF16),
            pltpu.VMEM((128, 5, 4, 128), BF16),
            pltpu.VMEM((128, 5, 4, 128), BF16),
            pltpu.VMEM((320, M), F32),
            pltpu.SemaphoreType.DMA((7,)),
            pltpu.SemaphoreType.DMA,
            pltpu.SemaphoreType.DMA((8,)),
        ],
        compiler_params=pltpu.CompilerParams(collective_id=0, has_side_effects=True, vmem_limit_bytes=32 << 20),
    )(*[pltpu.with_memory_space_constraint(v, pltpu.HBM) for v in (partners, waves, waves.reshape(8, 128), y, s, l)])


def dft_tables():
    a, lon = np.arange(128), np.arange(512)
    out = np.zeros((8, 256, 1024), np.float64)
    for b in range(8):
        angle = 2.0 * math.pi * (((8 * a + b)[:, None] * lon[None, :]) % NLON) / NLON
        cos, sin = np.cos(angle), np.sin(angle)
        out[b] = np.block([[cos, sin], [-sin, cos]])
    return out.astype(np.float32)


def grid_kernel(left, table, grid_hbm, slope_hbm, g, out, out_sem):
    for b in range(8):
        if b in (0, 4):
            g[b, :, pl.ds(0, 512)] = jnp.dot(left[b], table[b, :, pl.ds(0, 512)], preferred_element_type=F32)
        else:
            g[b] = jnp.dot(left[b], table[b], preferred_element_type=F32)

    root = math.sqrt(0.5)
    for n, target_hbm in enumerate((grid_hbm, slope_hbm)):

        def combine(i, carry, n=n, target_hbm=target_hbm):
            rows = pl.ds(pl.multiple_of(n * 160 + i * 16, 16), 16)
            for c in range(4):
                re = [g[b, rows, pl.ds(128 * c, 128)] for b in range(8)]
                im = [None if b in (0, 4) else g[b, rows, pl.ds(512 + 128 * c, 128)] for b in range(8)]
                plus, minus = re[0] + re[4], re[0] - re[4]
                r26, i26 = re[2] + re[6], im[6] - im[2]
                even = [plus + r26, minus + i26, plus - r26, minus - i26]
                r17, r35 = re[1] + re[7], re[3] + re[5]
                i71, i53 = im[7] - im[1], im[5] - im[3]
                rr, ii = root * (r17 - r35), root * (i71 + i53)
                odd = [r17 + r35, ii + rr, i71 - i53, ii - rr]
                for j in range(4):
                    out[rows, pl.ds(512 * j + 128 * c, 128)] = (even[j] + odd[j]).astype(BF16)
                    out[rows, pl.ds(512 * j + 2048 + 128 * c, 128)] = (even[j] - odd[j]).astype(BF16)
            pltpu.make_async_copy(out.at[rows], target_hbm.at[pl.ds(pl.multiple_of(i * 16, 16), 16)], out_sem.at[n]).start()
            return carry

        lax.fori_loop(0, 10, combine, 0)
    for n, target_hbm in enumerate((grid_hbm, slope_hbm)):
        pltpu.make_async_copy(out.at[pl.ds(160 * n, 160)], target_hbm, out_sem.at[n]).wait()


def to_grid(left, table):
    vmem = pl.BlockSpec(memory_space=pltpu.VMEM)
    hbm = pl.BlockSpec(memory_space=pltpu.HBM)
    shape = jax.ShapeDtypeStruct((160, NLON), BF16)
    return pl.pallas_call(
        grid_kernel,
        out_shape=(shape, shape),
        in_specs=[vmem, vmem],
        out_specs=(hbm, hbm),
        scratch_shapes=[
            pltpu.VMEM((8, 320, 1024), F32),
            pltpu.VMEM((320, NLON), BF16),
            pltpu.SemaphoreType.DMA((2,)),
        ],
        compiler_params=pltpu.CompilerParams(vmem_limit_bytes=32 << 20),
    )(left, table)


def body(coefficients, section_factors, level_factors, partners, wave_ids):
    y = coefficients.reshape(NW * NF, 2, 2, 4, 128).transpose(0, 2, 3, 1, 4).reshape(NW * NF * 16, 128)
    left = synth(partners, wave_ids, y, section_factors[0], level_factors[0])
    grid, slope = to_grid(left, jnp.asarray(dft_tables(), BF16))
    shape = (2, NF, 8, NLON)
    return (
        grid.reshape(shape).transpose(0, 2, 1, 3),
        slope.reshape(shape).transpose(0, 2, 1, 3),
    )


def solution(mesh):
    in_specs = (
        P("ha", "ma", None, None, None),
        P("ha", "ma", None, None),
        P("ha", None, "ma", None, None),
        P(),
        P(),
    )
    out_specs = (P(None, ("ma", "ha"), None, None), P(None, ("ma", "ha"), None, None))
    return jax.shard_map(body, mesh=mesh, in_specs=in_specs, out_specs=out_specs, check_vma=False)
```

```python
import functools
import math

import jax
import jax.numpy as jnp
import numpy as np
from jax import lax
from jax.experimental import pallas as pl
from jax.experimental.pallas import tpu as pltpu
from jax.sharding import PartitionSpec as P

NLON = 4096
K = 64
NB = 16
NW = 16
NF = 10
M = 1024
LANES = 384
F32 = jnp.float32
BF16 = jnp.bfloat16
MESH = pl.DeviceIdType.MESH
NT = (((1,), (1,)), ((), ()))
TILE_WAVES = ((0, 6), (6, 12), (12, 16))


def target(g):
    return {"ma": g // 2, "ha": g % 2}


def iota(shape, dim):
    return lax.broadcasted_iota(jnp.int32, shape, dim)


def keep_waves(block, masks):
    return jnp.concatenate([jnp.where(m, block, jnp.zeros_like(block)) for m in masks], axis=0)


ORDER = (7, 3, 5, 1, 6, 2, 4, 0)


def pick(bit, base):
    return 1 - base if bit else base


def mask_at(step, place):
    return ORDER[(step + 2 * place) % 8]


def synth_kernel(
    partners_hbm, waves_hbm, table_hbm, y_hbm, s_hbm, l_hbm, left,
    partners, waves, wave_rows, yv, yf, zin, z0, z1, sv, lv, perm, send, recv, onehot, acc, in_sem, send_sem, recv_sem,
):
    ma = lax.axis_index("ma")
    ha = lax.axis_index("ha")
    me = ma * 2 + ha
    slot = ha * 64 + ma

    loads = [
        pltpu.make_async_copy(y_hbm, yv, in_sem.at[0]),
        pltpu.make_async_copy(waves_hbm, waves, in_sem.at[1]),
        pltpu.make_async_copy(partners_hbm, partners, in_sem.at[2]),
        pltpu.make_async_copy(table_hbm, wave_rows, in_sem.at[3]),
        pltpu.make_async_copy(s_hbm, sv, in_sem.at[4]),
        pltpu.make_async_copy(l_hbm.at[0], lv.at[0], in_sem.at[5]),
    ]
    for load in loads:
        load.start()

    pair = me // 16
    low_bits = [me % 2, (me // 2) % 2, (me // 4) % 2, (me // 8) % 2]
    high = [pair % 2, (pair // 2) % 2, pair // 4]
    at_place = [pick(1 - (n & 1), low_bits[1]) * pick(1 - (n >> 1), low_bits[2]) for n in range(4)]

    def partner_pair(mask):
        return sum(pick((mask >> i) & 1, high[i]) * (1 << i) for i in range(3))

    order = [sum(at_place[n] * partner_pair(mask_at(i, n)) for n in range(4)) for i in range(8)]
    late_loads = []
    for i, p in enumerate(order):
        lanes = pl.ds(pl.multiple_of(p * 256, 256), 256)
        late_loads.append(pltpu.make_async_copy(l_hbm.at[1, :, :, lanes], lv.at[1, :, :, lanes], in_sem.at[6 + i]))

    barrier = pltpu.get_barrier_semaphore()

    def greet(first, last):
        for step in range(max(first, 1), last):
            pl.semaphore_signal(barrier, inc=1, device_id=target((me + step) % 128), device_id_type=MESH)

    col = iota((1, LANES), 1)
    col = jnp.where(col < 320, col, col - 64)
    wave = col % 16
    fr = col // 16
    tile = (wave >= 6).astype(jnp.int32) + (wave >= 12).astype(jnp.int32)
    source = tile * 128 + (fr % 2) * 64 + (wave - 6 * tile) * 10 + fr // 2
    perm[...] = (iota((LANES, LANES), 0) == source).astype(F32).astype(BF16)
    eye = (iota((128, 128), 0) == iota((128, 128), 1)).astype(F32).astype(BF16)
    lane_wave = (iota((128, 128), 1) % 64) // 10
    masks = [lane_wave == w for w in range(6)]

    yf[pl.ds(3840, 768), :] = jnp.zeros((768, 128), F32)
    degree = 2 * ((iota((16, 128), 0) // 2) * 128 + iota((16, 128), 1)) + ha
    greet(0, 64)
    loads[1].wait()
    loads[0].wait()
    for w in range(NW):
        keep = degree <= (M - 1) - waves[ma * NW + w]
        for f in range(NF):
            row = (w * NF + f) * 16
            yf[pl.ds((w * NF + f) * 24, 16), :] = jnp.where(keep, yv[pl.ds(row, 16), :].astype(F32), 0.0)
        greet(64 + 4 * w, 68 + 4 * w)
    for j in range(8):
        for t in range(3):
            rows = [yf[pl.ds(t * 1440 + 2 * j + part, 64, stride=24), :] for part in range(2)]
            block = jnp.concatenate(rows, axis=0).astype(BF16)
            turned = lax.dot_general(eye, block, NT, preferred_element_type=F32)
            zin[j, :, pl.ds(t * 128, 128)] = turned.astype(BF16)

    loads[4].wait()
    for load in late_loads:
        load.start()
    half_masks = [m[:64] for m in masks]

    def section(j, carry):
        lanes = pl.ds(pl.multiple_of(j * 128, 128), 128)
        for t, (first, last) in enumerate(TILE_WAVES):
            for k in range(2):
                side = slice(64 * k, 64 * k + 64)
                factors = jnp.concatenate([sv[w, :, lanes][:, side] for w in range(first, last)], axis=1)
                right = keep_waves(zin[j, pl.ds(64 * k, 64), pl.ds(t * 128, 128)], half_masks[: last - first])
                out = jnp.dot(factors, right, preferred_element_type=F32)
                z0[2 * j + k, :, pl.ds(t * 128, 128)] = out.astype(BF16)
        return carry

    lax.fori_loop(0, 8, section, 0, unroll=2)

    def level(l, b, own_state, other_state):
        lanes = pl.ds(pl.multiple_of(b * 128, 128), 128)
        outs = []
        for t, (first, last) in enumerate(TILE_WAVES):
            factors = jnp.concatenate([lv[l, w, :, lanes] for w in range(first, last)], axis=1)
            right = keep_waves(jnp.concatenate([own_state[t], other_state[t]], axis=0), masks[: last - first])
            outs.append(jnp.dot(factors, right, preferred_element_type=F32).astype(BF16))
        return outs

    def tiles(z, b):
        return [z[b, :, pl.ds(t * 128, 128)] for t in range(3)]

    def first_level(b, carry):
        for t, out in enumerate(level(0, b, tiles(z0, b), tiles(z0, partners[0, b]))):
            z1[b, :, pl.ds(t * 128, 128)] = out
        return carry

    loads[2].wait()
    loads[3].wait()
    loads[5].wait()
    lax.fori_loop(0, NB, first_level, 0, unroll=8)
    half = iota((16, 4, 128), 2) < 64

    at_place = [pick(1 - (n & 1), low_bits[1]) * pick(1 - (n >> 1), low_bits[2]) for n in range(4)]

    def partner_pair(mask):
        return sum(pick((mask >> i) & 1, high[i]) * (1 << i) for i in range(3))

    for i, p in enumerate(order):
        own = p == pair
        late_loads[i].wait()
        blocks = [level(1, 2 * p + k, tiles(z1, 2 * p + k), tiles(z1, partners[1, 2 * p + k])) for k in range(2)]
        if i == 0:
            pl.semaphore_wait(barrier, 127)
        state = jnp.concatenate([jnp.concatenate(outs, axis=1) for outs in blocks], axis=0)
        moved = jnp.dot(state, perm[...], preferred_element_type=F32)
        groups = pl.ds(p * 16, 16)
        for t in range(3):
            rows = moved[:, t * 128 : (t + 1) * 128].reshape(16, 8, 128)
            if t < 2:
                send[groups, 2 * t] = rows[:, :4].astype(BF16)
                send[groups, 2 * t + 1] = rows[:, 4:].astype(BF16)
            else:
                send[groups, 4] = jnp.where(half, rows[:, :4], rows[:, 4:]).astype(BF16)
        for r in range(15, -1, -1):
            g = p * 16 + sum(pick((r >> n) & 1, low_bits[n]) * (1 << n) for n in range(4))

            def go():
                pltpu.make_async_remote_copy(
                    send.at[g], recv.at[slot], send_sem, recv_sem.at[i], device_id=target(g), device_id_type=MESH
                ).start()

            if r == 0:
                pl.when(jnp.logical_not(own))(go)
                pl.when(own)(pltpu.make_async_copy(send.at[g], recv.at[slot], recv_sem.at[i]).start)
            else:
                go()

    group = iota((8, 128), 1) // 16
    lane_place = (iota((1, 128), 1) // 16) % 4
    row = iota((M, 1), 0)
    k = 8 * (row % 128) + row // 128
    weight = jnp.where(k > 0, 2.0, 1.0)
    for i in range(8):
        pairs = [partner_pair(mask_at(i, n)) for n in range(4)]
        slot_wave = wave_rows[pl.ds(pairs[0], 1), :]
        for n in range(1, 4):
            slot_wave = jnp.where(lane_place == n, wave_rows[pl.ds(pairs[n], 1), :], slot_wave)
        onehot[i] = jnp.where(slot_wave == k, weight, 0.0).astype(BF16)

    for i in range(8):
        pairs = [partner_pair(mask_at(i, n)) for n in range(4)]
        pltpu.make_async_remote_copy(
            send.at[pl.ds(0, 16)], recv.at[pl.ds(0, 16)], send_sem, recv_sem.at[i],
            device_id=target(me), device_id_type=MESH,
        ).wait_recv()
        parts = [[None] * 20, [None] * 20]
        for q in range(3):
            sides = []
            for p in range(2):
                rows = []
                for n in range(8):
                    message = recv.at[p * 64 + 8 * pairs[n % 4] + n]
                    if q < 2:
                        rows.append(jnp.concatenate([message[2 * q].astype(F32), message[2 * q + 1].astype(F32)], axis=0))
                    else:
                        packed = message[4].astype(F32)
                        both = jnp.concatenate([packed, packed], axis=0)
                        rows.append(jnp.where(iota((8, 128), 0) < 4, both, pltpu.roll(both, 64, 1)))
                for d in (4, 2, 1):
                    upper = (group // d) % 2 == 1
                    new = list(rows)
                    for n in range(len(rows)):
                        if n & d or n + d >= len(rows):
                            continue
                        one, two = rows[n], rows[n + d]
                        new[n] = jnp.where(upper, pltpu.roll(two, 16 * d, 1), one)
                        new[n + d] = jnp.where(upper, two, pltpu.roll(one, 128 - 16 * d, 1))
                    rows = new
                    if q == 2 and d == 4:
                        rows = rows[:4]
                sides.append(rows)
            for n, (even, odd) in enumerate(zip(*sides)):
                fr = q * 8 + n
                parts[fr % 2][fr // 2] = even + odd
                parts[fr % 2][10 + fr // 2] = even - odd
        spectra = jnp.concatenate(parts[0] + parts[1], axis=0).astype(BF16)
        for b in range(8):
            lanes = pl.ds(b * 128, 128)
            moved = lax.dot_general(spectra, onehot[i, pl.ds(b * 128, 128), :], NT, preferred_element_type=F32)
            if i > 0:
                moved = moved + acc[:, lanes]
            if i < 7:
                acc[:, lanes] = moved
            else:
                real, imag = moved[:160], moved[160:]
                scale = (8 * iota((1, 128), 1) + b).astype(F32) * (1.0 / M)
                left[b, pl.ds(0, 160), pl.ds(0, 128)] = real.astype(BF16)
                left[b, pl.ds(0, 160), pl.ds(128, 128)] = imag.astype(BF16)
                left[b, pl.ds(160, 160), pl.ds(0, 128)] = (-scale * imag).astype(BF16)
                left[b, pl.ds(160, 160), pl.ds(128, 128)] = (scale * real).astype(BF16)

    pltpu.make_async_remote_copy(
        send.at[pl.ds(0, 127)], recv.at[pl.ds(0, 127)], send_sem, recv_sem.at[0], device_id=target(me), device_id_type=MESH
    ).wait_send()


def synth(partners, waves, y, s, l):
    hbm = pl.BlockSpec(memory_space=pltpu.HBM)
    return pl.pallas_call(
        synth_kernel,
        out_shape=jax.ShapeDtypeStruct((8, 320, 256), BF16),
        in_specs=[hbm] * 6,
        out_specs=pl.BlockSpec(memory_space=pltpu.VMEM),
        scratch_shapes=[
            pltpu.SMEM((2, NB), jnp.int32),
            pltpu.SMEM((M,), jnp.int32),
            pltpu.VMEM((8, 128), jnp.int32),
            pltpu.VMEM((2560, 128), BF16),
            pltpu.VMEM((4608, 128), F32),
            pltpu.VMEM((8, 128, LANES), BF16),
            pltpu.VMEM((NB, K, LANES), BF16),
            pltpu.VMEM((NB, K, LANES), BF16),
            pltpu.VMEM((NW, K, 1024), BF16),
            pltpu.VMEM((2, NW, K, 2048), BF16),
            pltpu.VMEM((LANES, LANES), BF16),
            pltpu.VMEM((128, 5, 4, 128), BF16),
            pltpu.VMEM((128, 5, 4, 128), BF16),
            pltpu.VMEM((8, M, 128), BF16),
            pltpu.VMEM((320, M), F32),
            pltpu.SemaphoreType.DMA((14,)),
            pltpu.SemaphoreType.DMA,
            pltpu.SemaphoreType.DMA((8,)),
        ],
        compiler_params=pltpu.CompilerParams(collective_id=0, has_side_effects=True, vmem_limit_bytes=32 << 20),
    )(*[pltpu.with_memory_space_constraint(v, pltpu.HBM) for v in (partners, waves, waves.reshape(8, 128), y, s, l)])


def dft_tables():
    a, lon = np.arange(128), np.arange(512)
    out = np.zeros((8, 256, 1024), np.float64)
    for b in range(8):
        angle = 2.0 * math.pi * (((8 * a + b)[:, None] * lon[None, :]) % NLON) / NLON
        cos, sin = np.cos(angle), np.sin(angle)
        out[b] = np.block([[cos, sin], [-sin, cos]])
    return out.astype(np.float32)


def grid_kernel(left, table, grid_hbm, slope_hbm, g, out, out_sem):
    for b in range(8):
        if b in (0, 4):
            g[b, :, pl.ds(0, 512)] = jnp.dot(left[b], table[b, :, pl.ds(0, 512)], preferred_element_type=F32)
        else:
            g[b] = jnp.dot(left[b], table[b], preferred_element_type=F32)

    root = math.sqrt(0.5)
    for n, target_hbm in enumerate((grid_hbm, slope_hbm)):

        def combine(i, carry, n=n, target_hbm=target_hbm):
            rows = pl.ds(pl.multiple_of(n * 160 + i * 16, 16), 16)
            for c in range(4):
                re = [g[b, rows, pl.ds(128 * c, 128)] for b in range(8)]
                im = [None if b in (0, 4) else g[b, rows, pl.ds(512 + 128 * c, 128)] for b in range(8)]
                plus, minus = re[0] + re[4], re[0] - re[4]
                r26, i26 = re[2] + re[6], im[6] - im[2]
                even = [plus + r26, minus + i26, plus - r26, minus - i26]
                r17, r35 = re[1] + re[7], re[3] + re[5]
                i71, i53 = im[7] - im[1], im[5] - im[3]
                rr, ii = root * (r17 - r35), root * (i71 + i53)
                odd = [r17 + r35, ii + rr, i71 - i53, ii - rr]
                for j in range(4):
                    out[rows, pl.ds(512 * j + 128 * c, 128)] = (even[j] + odd[j]).astype(BF16)
                    out[rows, pl.ds(512 * j + 2048 + 128 * c, 128)] = (even[j] - odd[j]).astype(BF16)
            pltpu.make_async_copy(out.at[rows], target_hbm.at[pl.ds(pl.multiple_of(i * 16, 16), 16)], out_sem.at[n]).start()
            return carry

        lax.fori_loop(0, 10, combine, 0, unroll=2)
    for n, target_hbm in enumerate((grid_hbm, slope_hbm)):
        pltpu.make_async_copy(out.at[pl.ds(160 * n, 160)], target_hbm, out_sem.at[n]).wait()


def to_grid(left, table):
    vmem = pl.BlockSpec(memory_space=pltpu.VMEM)
    hbm = pl.BlockSpec(memory_space=pltpu.HBM)
    shape = jax.ShapeDtypeStruct((160, NLON), BF16)
    return pl.pallas_call(
        grid_kernel,
        out_shape=(shape, shape),
        in_specs=[vmem, vmem],
        out_specs=(hbm, hbm),
        scratch_shapes=[
            pltpu.VMEM((8, 320, 1024), F32),
            pltpu.VMEM((320, NLON), BF16),
            pltpu.SemaphoreType.DMA((2,)),
        ],
        compiler_params=pltpu.CompilerParams(vmem_limit_bytes=32 << 20),
    )(left, table)


def body(coefficients, section_factors, level_factors, partners, wave_ids):
    y = coefficients.reshape(NW * NF, 2, 2, 4, 128).transpose(0, 2, 3, 1, 4).reshape(NW * NF * 16, 128)
    left = synth(partners, wave_ids, y, section_factors[0], level_factors[0])
    grid, slope = to_grid(left, jnp.asarray(dft_tables(), BF16))
    shape = (2, NF, 8, NLON)
    return (
        grid.reshape(shape).transpose(0, 2, 1, 3),
        slope.reshape(shape).transpose(0, 2, 1, 3),
    )


def solution(mesh):
    in_specs = (
        P("ha", "ma", None, None, None),
        P("ha", "ma", None, None),
        P("ha", None, "ma", None, None),
        P(),
        P(),
    )
    out_specs = (P(None, ("ma", "ha"), None, None), P(None, ("ma", "ha"), None, None))
    return jax.shard_map(body, mesh=mesh, in_specs=in_specs, out_specs=out_specs, check_vma=False)
```

```python
import functools
import math

import jax
import jax.numpy as jnp
import numpy as np
from jax import lax
from jax.experimental import pallas as pl
from jax.experimental.pallas import tpu as pltpu
from jax.sharding import PartitionSpec as P

NLON = 4096
K = 64
NB = 16
NW = 16
NF = 10
M = 1024
LANES = 384
F32 = jnp.float32
BF16 = jnp.bfloat16
MESH = pl.DeviceIdType.MESH
NT = (((1,), (1,)), ((), ()))
TILE_WAVES = ((0, 6), (6, 12), (12, 16))


def target(g):
    return {"ma": g // 2, "ha": g % 2}


def iota(shape, dim):
    return lax.broadcasted_iota(jnp.int32, shape, dim)


def keep_waves(block, masks):
    return jnp.concatenate([jnp.where(m, block, jnp.zeros_like(block)) for m in masks], axis=0)


ORDER = (7, 3, 5, 1, 6, 2, 4, 0)


def pick(bit, base):
    return 1 - base if bit else base


def mask_at(step, place):
    return ORDER[(step + (0, 4, 1, 5)[place]) % 8]


def synth_kernel(
    partners_hbm, waves_hbm, table_hbm, y_hbm, s_hbm, l_hbm, left,
    partners, waves, wave_rows, yv, yf, zin, z0, z1, sv, lv, perm, send, recv, onehot, acc, in_sem, send_sem, recv_sem,
):
    ma = lax.axis_index("ma")
    ha = lax.axis_index("ha")
    me = ma * 2 + ha
    slot = ha * 64 + ma

    loads = [
        pltpu.make_async_copy(y_hbm, yv, in_sem.at[0]),
        pltpu.make_async_copy(waves_hbm, waves, in_sem.at[1]),
        pltpu.make_async_copy(partners_hbm, partners, in_sem.at[2]),
        pltpu.make_async_copy(table_hbm, wave_rows, in_sem.at[3]),
        pltpu.make_async_copy(s_hbm, sv, in_sem.at[4]),
        pltpu.make_async_copy(l_hbm.at[0], lv.at[0], in_sem.at[5]),
    ]
    for load in loads:
        load.start()

    pair = me // 16
    low_bits = [me % 2, (me // 2) % 2, (me // 4) % 2, (me // 8) % 2]
    high = [pair % 2, (pair // 2) % 2, pair // 4]
    at_place = [pick(1 - (n & 1), low_bits[1]) * pick(1 - (n >> 1), low_bits[2]) for n in range(4)]

    def partner_pair(mask):
        return sum(pick((mask >> i) & 1, high[i]) * (1 << i) for i in range(3))

    order = [sum(at_place[n] * partner_pair(mask_at(i, n)) for n in range(4)) for i in range(8)]
    late_loads = []
    for i, p in enumerate(order):
        lanes = pl.ds(pl.multiple_of(p * 256, 256), 256)
        late_loads.append(pltpu.make_async_copy(l_hbm.at[1, :, :, lanes], lv.at[1, :, :, lanes], in_sem.at[6 + i]))

    barrier = pltpu.get_barrier_semaphore()

    def greet(first, last):
        for step in range(max(first, 1), last):
            pl.semaphore_signal(barrier, inc=1, device_id=target((me + step) % 128), device_id_type=MESH)

    col = iota((1, LANES), 1)
    col = jnp.where(col < 320, col, col - 64)
    wave = col % 16
    fr = col // 16
    tile = (wave >= 6).astype(jnp.int32) + (wave >= 12).astype(jnp.int32)
    source = tile * 128 + (fr % 2) * 64 + (wave - 6 * tile) * 10 + fr // 2
    perm[...] = (iota((LANES, LANES), 0) == source).astype(F32).astype(BF16)
    eye = (iota((128, 128), 0) == iota((128, 128), 1)).astype(F32).astype(BF16)
    lane_wave = (iota((128, 128), 1) % 64) // 10
    masks = [lane_wave == w for w in range(6)]

    yf[pl.ds(3840, 768), :] = jnp.zeros((768, 128), F32)
    degree = 2 * ((iota((16, 128), 0) // 2) * 128 + iota((16, 128), 1)) + ha
    greet(0, 64)
    loads[1].wait()
    loads[0].wait()
    for w in range(NW):
        keep = degree <= (M - 1) - waves[ma * NW + w]
        for f in range(NF):
            row = (w * NF + f) * 16
            yf[pl.ds((w * NF + f) * 24, 16), :] = jnp.where(keep, yv[pl.ds(row, 16), :].astype(F32), 0.0)
        greet(64 + 4 * w, 68 + 4 * w)
    for j in range(8):
        for t in range(3):
            rows = [yf[pl.ds(t * 1440 + 2 * j + part, 64, stride=24), :] for part in range(2)]
            block = jnp.concatenate(rows, axis=0).astype(BF16)
            turned = lax.dot_general(eye, block, NT, preferred_element_type=F32)
            zin[j, :, pl.ds(t * 128, 128)] = turned.astype(BF16)

    loads[4].wait()
    for load in late_loads:
        load.start()
    half_masks = [m[:64] for m in masks]

    def section(j, carry):
        lanes = pl.ds(pl.multiple_of(j * 128, 128), 128)
        for t, (first, last) in enumerate(TILE_WAVES):
            for k in range(2):
                side = slice(64 * k, 64 * k + 64)
                factors = jnp.concatenate([sv[w, :, lanes][:, side] for w in range(first, last)], axis=1)
                right = keep_waves(zin[j, pl.ds(64 * k, 64), pl.ds(t * 128, 128)], half_masks[: last - first])
                out = jnp.dot(factors, right, preferred_element_type=F32)
                z0[2 * j + k, :, pl.ds(t * 128, 128)] = out.astype(BF16)
        return carry

    lax.fori_loop(0, 8, section, 0, unroll=2)

    def level(l, b, own_state, other_state):
        lanes = pl.ds(pl.multiple_of(b * 128, 128), 128)
        outs = []
        for t, (first, last) in enumerate(TILE_WAVES):
            factors = jnp.concatenate([lv[l, w, :, lanes] for w in range(first, last)], axis=1)
            right = keep_waves(jnp.concatenate([own_state[t], other_state[t]], axis=0), masks[: last - first])
            outs.append(jnp.dot(factors, right, preferred_element_type=F32).astype(BF16))
        return outs

    def tiles(z, b):
        return [z[b, :, pl.ds(t * 128, 128)] for t in range(3)]

    def first_level(b, carry):
        for t, out in enumerate(level(0, b, tiles(z0, b), tiles(z0, partners[0, b]))):
            z1[b, :, pl.ds(t * 128, 128)] = out
        return carry

    loads[2].wait()
    loads[3].wait()
    loads[5].wait()
    lax.fori_loop(0, NB, first_level, 0, unroll=8)
    half = iota((16, 4, 128), 2) < 64

    at_place = [pick(1 - (n & 1), low_bits[1]) * pick(1 - (n >> 1), low_bits[2]) for n in range(4)]

    def partner_pair(mask):
        return sum(pick((mask >> i) & 1, high[i]) * (1 << i) for i in range(3))

    for i, p in enumerate(order):
        own = p == pair
        late_loads[i].wait()
        blocks = [level(1, 2 * p + k, tiles(z1, 2 * p + k), tiles(z1, partners[1, 2 * p + k])) for k in range(2)]
        if i == 0:
            pl.semaphore_wait(barrier, 127)
        state = jnp.concatenate([jnp.concatenate(outs, axis=1) for outs in blocks], axis=0)
        moved = jnp.dot(state, perm[...], preferred_element_type=F32)
        groups = pl.ds(p * 16, 16)
        for t in range(3):
            rows = moved[:, t * 128 : (t + 1) * 128].reshape(16, 8, 128)
            if t < 2:
                send[groups, 2 * t] = rows[:, :4].astype(BF16)
                send[groups, 2 * t + 1] = rows[:, 4:].astype(BF16)
            else:
                send[groups, 4] = jnp.where(half, rows[:, :4], rows[:, 4:]).astype(BF16)
        for r in (9, 1, 11, 3, 13, 5, 15, 7, 8, 10, 2, 12, 4, 14, 6, 0):
            g = p * 16 + sum(pick((r >> n) & 1, low_bits[n]) * (1 << n) for n in range(4))

            def go():
                pltpu.make_async_remote_copy(
                    send.at[g], recv.at[slot], send_sem, recv_sem.at[i], device_id=target(g), device_id_type=MESH
                ).start()

            if r == 0:
                pl.when(jnp.logical_not(own))(go)
                pl.when(own)(pltpu.make_async_copy(send.at[g], recv.at[slot], recv_sem.at[i]).start)
            else:
                go()

    group = iota((8, 128), 1) // 16
    lane_place = (iota((1, 128), 1) // 16) % 4
    row = iota((M, 1), 0)
    k = 8 * (row % 128) + row // 128
    weight = jnp.where(k > 0, 2.0, 1.0)
    for i in range(8):
        pairs = [partner_pair(mask_at(i, n)) for n in range(4)]
        slot_wave = wave_rows[pl.ds(pairs[0], 1), :]
        for n in range(1, 4):
            slot_wave = jnp.where(lane_place == n, wave_rows[pl.ds(pairs[n], 1), :], slot_wave)
        onehot[i] = jnp.where(slot_wave == k, weight, 0.0).astype(BF16)

    for i in range(8):
        pairs = [partner_pair(mask_at(i, n)) for n in range(4)]
        pltpu.make_async_remote_copy(
            send.at[pl.ds(0, 16)], recv.at[pl.ds(0, 16)], send_sem, recv_sem.at[i],
            device_id=target(me), device_id_type=MESH,
        ).wait_recv()
        parts = [[None] * 20, [None] * 20]
        for q in range(3):
            sides = []
            for p in range(2):
                rows = []
                for n in range(8):
                    message = recv.at[p * 64 + 8 * pairs[n % 4] + n]
                    if q < 2:
                        rows.append(jnp.concatenate([message[2 * q].astype(F32), message[2 * q + 1].astype(F32)], axis=0))
                    else:
                        packed = message[4].astype(F32)
                        both = jnp.concatenate([packed, packed], axis=0)
                        rows.append(jnp.where(iota((8, 128), 0) < 4, both, pltpu.roll(both, 64, 1)))
                for d in (4, 2, 1):
                    upper = (group // d) % 2 == 1
                    new = list(rows)
                    for n in range(len(rows)):
                        if n & d or n + d >= len(rows):
                            continue
                        one, two = rows[n], rows[n + d]
                        new[n] = jnp.where(upper, pltpu.roll(two, 16 * d, 1), one)
                        new[n + d] = jnp.where(upper, two, pltpu.roll(one, 128 - 16 * d, 1))
                    rows = new
                    if q == 2 and d == 4:
                        rows = rows[:4]
                sides.append(rows)
            for n, (even, odd) in enumerate(zip(*sides)):
                fr = q * 8 + n
                parts[fr % 2][fr // 2] = even + odd
                parts[fr % 2][10 + fr // 2] = even - odd
        spectra = jnp.concatenate(parts[0] + parts[1], axis=0).astype(BF16)
        for b in range(8):
            lanes = pl.ds(b * 128, 128)
            moved = lax.dot_general(spectra, onehot[i, pl.ds(b * 128, 128), :], NT, preferred_element_type=F32)
            if i > 0:
                moved = moved + acc[:, lanes]
            if i < 7:
                acc[:, lanes] = moved
            else:
                real, imag = moved[:160], moved[160:]
                scale = (8 * iota((1, 128), 1) + b).astype(F32) * (1.0 / M)
                left[b, pl.ds(0, 160), pl.ds(0, 128)] = real.astype(BF16)
                left[b, pl.ds(0, 160), pl.ds(128, 128)] = imag.astype(BF16)
                left[b, pl.ds(160, 160), pl.ds(0, 128)] = (-scale * imag).astype(BF16)
                left[b, pl.ds(160, 160), pl.ds(128, 128)] = (scale * real).astype(BF16)

    pltpu.make_async_remote_copy(
        send.at[pl.ds(0, 127)], recv.at[pl.ds(0, 127)], send_sem, recv_sem.at[0], device_id=target(me), device_id_type=MESH
    ).wait_send()


def synth(partners, waves, y, s, l):
    hbm = pl.BlockSpec(memory_space=pltpu.HBM)
    return pl.pallas_call(
        synth_kernel,
        out_shape=jax.ShapeDtypeStruct((8, 320, 256), BF16),
        in_specs=[hbm] * 6,
        out_specs=pl.BlockSpec(memory_space=pltpu.VMEM),
        scratch_shapes=[
            pltpu.SMEM((2, NB), jnp.int32),
            pltpu.SMEM((M,), jnp.int32),
            pltpu.VMEM((8, 128), jnp.int32),
            pltpu.VMEM((2560, 128), BF16),
            pltpu.VMEM((4608, 128), F32),
            pltpu.VMEM((8, 128, LANES), BF16),
            pltpu.VMEM((NB, K, LANES), BF16),
            pltpu.VMEM((NB, K, LANES), BF16),
            pltpu.VMEM((NW, K, 1024), BF16),
            pltpu.VMEM((2, NW, K, 2048), BF16),
            pltpu.VMEM((LANES, LANES), BF16),
            pltpu.VMEM((128, 5, 4, 128), BF16),
            pltpu.VMEM((128, 5, 4, 128), BF16),
            pltpu.VMEM((8, M, 128), BF16),
            pltpu.VMEM((320, M), F32),
            pltpu.SemaphoreType.DMA((14,)),
            pltpu.SemaphoreType.DMA,
            pltpu.SemaphoreType.DMA((8,)),
        ],
        compiler_params=pltpu.CompilerParams(collective_id=0, has_side_effects=True, vmem_limit_bytes=32 << 20),
    )(*[pltpu.with_memory_space_constraint(v, pltpu.HBM) for v in (partners, waves, waves.reshape(8, 128), y, s, l)])


def dft_tables():
    a, lon = np.arange(128), np.arange(512)
    out = np.zeros((8, 256, 1024), np.float64)
    for b in range(8):
        angle = 2.0 * math.pi * (((8 * a + b)[:, None] * lon[None, :]) % NLON) / NLON
        cos, sin = np.cos(angle), np.sin(angle)
        out[b] = np.block([[cos, sin], [-sin, cos]])
    return out.astype(np.float32)


def grid_kernel(left, table, grid_hbm, slope_hbm, g, out, out_sem):
    for b in range(8):
        if b in (0, 4):
            g[b, :, pl.ds(0, 512)] = jnp.dot(left[b], table[b, :, pl.ds(0, 512)], preferred_element_type=F32)
        else:
            g[b] = jnp.dot(left[b], table[b], preferred_element_type=F32)

    root = math.sqrt(0.5)
    for n, target_hbm in enumerate((grid_hbm, slope_hbm)):

        def combine(i, carry, n=n, target_hbm=target_hbm):
            rows = pl.ds(pl.multiple_of(n * 160 + i * 16, 16), 16)
            for c in range(4):
                re = [g[b, rows, pl.ds(128 * c, 128)] for b in range(8)]
                im = [None if b in (0, 4) else g[b, rows, pl.ds(512 + 128 * c, 128)] for b in range(8)]
                plus, minus = re[0] + re[4], re[0] - re[4]
                r26, i26 = re[2] + re[6], im[6] - im[2]
                even = [plus + r26, minus + i26, plus - r26, minus - i26]
                r17, r35 = re[1] + re[7], re[3] + re[5]
                i71, i53 = im[7] - im[1], im[5] - im[3]
                rr, ii = root * (r17 - r35), root * (i71 + i53)
                odd = [r17 + r35, ii + rr, i71 - i53, ii - rr]
                for j in range(4):
                    out[rows, pl.ds(512 * j + 128 * c, 128)] = (even[j] + odd[j]).astype(BF16)
                    out[rows, pl.ds(512 * j + 2048 + 128 * c, 128)] = (even[j] - odd[j]).astype(BF16)
            pltpu.make_async_copy(out.at[rows], target_hbm.at[pl.ds(pl.multiple_of(i * 16, 16), 16)], out_sem.at[n]).start()
            return carry

        lax.fori_loop(0, 10, combine, 0, unroll=5)
    for n, target_hbm in enumerate((grid_hbm, slope_hbm)):
        pltpu.make_async_copy(out.at[pl.ds(160 * n, 160)], target_hbm, out_sem.at[n]).wait()


def to_grid(left, table):
    vmem = pl.BlockSpec(memory_space=pltpu.VMEM)
    hbm = pl.BlockSpec(memory_space=pltpu.HBM)
    shape = jax.ShapeDtypeStruct((160, NLON), BF16)
    return pl.pallas_call(
        grid_kernel,
        out_shape=(shape, shape),
        in_specs=[vmem, vmem],
        out_specs=(hbm, hbm),
        scratch_shapes=[
            pltpu.VMEM((8, 320, 1024), F32),
            pltpu.VMEM((320, NLON), BF16),
            pltpu.SemaphoreType.DMA((2,)),
        ],
        compiler_params=pltpu.CompilerParams(vmem_limit_bytes=32 << 20),
    )(left, table)


def body(coefficients, section_factors, level_factors, partners, wave_ids):
    y = coefficients.reshape(NW * NF, 2, 2, 4, 128).transpose(0, 2, 3, 1, 4).reshape(NW * NF * 16, 128)
    left = synth(partners, wave_ids, y, section_factors[0], level_factors[0])
    grid, slope = to_grid(left, jnp.asarray(dft_tables(), BF16))
    shape = (2, NF, 8, NLON)
    return (
        grid.reshape(shape).transpose(0, 2, 1, 3),
        slope.reshape(shape).transpose(0, 2, 1, 3),
    )


def solution(mesh):
    in_specs = (
        P("ha", "ma", None, None, None),
        P("ha", "ma", None, None),
        P("ha", None, "ma", None, None),
        P(),
        P(),
    )
    out_specs = (P(None, ("ma", "ha"), None, None), P(None, ("ma", "ha"), None, None))
    return jax.shard_map(body, mesh=mesh, in_specs=in_specs, out_specs=out_specs, check_vma=False)
```
